32 devices in a mesh: groups: 2 (over x), node: 8 (over z, y), local: 2 (over core).
Axes of the slice: x: 2, y: 2, z: 4, core: 2. Of those that a mesh axis runs over, the one named last changes fastest.
Arguments:
- hidden_rows: bfloat16 [256, 7168], P(('groups', 'node', 'local')), parts along dimension 0, may hold values from -6 to 6
- expert_ids: int32 [256, 2], P(('groups', 'node', 'local')), parts along dimension 0, may hold values from 0 to 3, all different within a row; in each aligned block of 8 rows (0 to 7, 8 to 15, ...) at most 6 rows name the same one
- gate_values: float32 [256, 2], P(('groups', 'node', 'local')), parts along dimension 0, may hold values from 0.1 to 1
- expert_block: int32 [4], replicated, may hold values from 0 to 3, each once
- w_gate: bfloat16 [7168, 4096], P(None, ('node', 'local')), may hold values from -0.0625 to 0.0625
- w_up: bfloat16 [7168, 4096], P(None, ('node', 'local')), may hold values from -0.0625 to 0.0625
- w_down: bfloat16 [4096, 7168], P(('node', 'local')), may hold values from -0.1875 to 0.1875
Outputs:
- combined: bfloat16 [256, 7168], P(('groups', 'node', 'local')), parts along dimension 0
The draws below stay inside these ranges and needn't reach their ends.
There are 2 independent parts, one for each index of `groups`. The reference program is written for one: setup_inputs(seed, part) draws one part's arguments, and reference() takes and returns one part's arrays. A program takes and returns all parts, laid end to end along the dimension named above; an argument that names none is the same for every part. Nothing has to cross between parts.
Inputs may be any that keep to these rules, and one draw needn't show every extreme that they name: `expert_ids`: each row names 2 different experts; among the rows of one device no expert is named by more than 6 pairs, and in every draw some device names some expert exactly 6 times. `expert_block`: A permutation of the experts.
All inputs are finite; a program needn't handle non-finite values.
Results may differ from the reference program's by a relative error of at most 0.0065.
Values may be sent and summed in bfloat16 or wider, within the bound.
A program may use at most 64 MiB of HBM per device.

```python
import math
import jax
import jax.numpy as jnp
import numpy as np
from jax import lax

D = 7168
FFE = 1024
ROW_DEV = 8
QUARTER = 256
EXPERTS = 4
TOP = 2
CAP = 6
ROWS = 128
N_NODE = 8
N_LOCAL = 2


def levels(rng, shape, split, smallest, high):
    loudness = 1.0
    for dim, shards_of in split:
        steps = jax.random.uniform(jax.random.fold_in(jax.random.fold_in(rng, 6), dim), (shards_of,), jnp.float32, smallest / len(split), high / len(split))
        loudness = loudness * jnp.repeat(jnp.exp(steps), shape[dim] // shards_of).reshape((-1,) + (1,) * (len(shape) - 1 - dim))
    return loudness


def routed_block(own_key, own, number, rows, amount, top, bound, slope):
    order = jax.random.permutation(own_key, amount)
    packed, common = portions_of(amount, rows * top, bound, slope, True), portions_of(amount, rows * top, bound, slope, False)
    places = jnp.arange(amount)

    def named(lengths, offset_by):
        used = int((lengths > 0).sum())
        fixed = max(1, used // 4)
        passed = fixed + (places - fixed + offset_by * (used - fixed)) % max(1, amount - fixed)
        return jnp.zeros((amount,), jnp.int32).at[order[jnp.where(places < fixed, places, passed)]].set(jnp.asarray(lengths, jnp.int32))

    lengths = jnp.where(number % 4 == 0, named(packed, number // 4), named(common, number - number // 4 - 1))
    mixed = jax.random.permutation(jax.random.fold_in(own, 3), amount)
    donor, sink = mixed[0:amount // 2 * 2:2], mixed[1:amount // 2 * 2:2]
    room = jnp.minimum(lengths[donor] - 1, bound - lengths[sink]) // 2
    room = jnp.where((donor == order[0]) | (sink == order[0]) | (lengths[sink] == 0), 0, jnp.maximum(room, 0))
    passed = jax.random.randint(jax.random.fold_in(own, 4), (amount // 2,), 0, 1 << 20) % (room + 1)
    lengths = lengths.at[donor].add(-passed).at[sink].add(passed)
    members = jnp.searchsorted(jnp.cumsum(lengths), jnp.arange(rows * top), side="right").astype(jnp.int32)
    table = members.reshape(top, rows).T
    table = table[jax.random.permutation(jax.random.fold_in(own, 1), rows)]
    offset_by = jax.random.randint(jax.random.fold_in(own, 2), (rows, 1), 0, top)
    return jnp.take_along_axis(table, (jnp.arange(top)[None, :] + offset_by) % top, axis=1)


def portions_of(count, total, limit, slope, full):
    loads = [(1 << 20) // math.isqrt(standing ** slope) + 1 for standing in range(1, count + 1)]
    largest = limit if full else min(limit, max(-(-total // count), total * loads[0] // sum(loads)))
    least = 1 if total - largest >= count - 1 else 0
    holding, rest = [largest] + [least] * (count - 1), total - largest - least * (count - 1)
    while rest > 0:
        movable = [i for i in range(1, count) if holding[i] < largest] or [i for i in range(1, count) if holding[i] < limit]
        whole, budget = sum([loads[i] for i in movable]), rest
        for i in movable:
            addition = min(limit - holding[i], max(1, budget * loads[i] // whole), rest)
            holding[i] = holding[i] + addition
            rest = rest - addition
    return np.array(holding)


def scatter_about(key, shape, deviation, limit, shards=(), held_as=jnp.bfloat16):
    values = jax.random.normal(key, shape, jnp.float32) * deviation
    if len(shards) > 0:
        values = levels(key, shape, shards, -0.22, 0.18) * values
    return jnp.clip(values, min=-limit, max=limit).astype(held_as)


def setup_inputs(seed: int = 0, part: int = 0) -> dict:
    streams_of = jax.random.split(jax.random.key(seed), 8)
    part_keys = jax.random.split(jax.random.fold_in(streams_of[7], part), 8)
    hidden_rows = scatter_about(part_keys[0], (ROWS, D), 1.0, 6.0, ((0, 16),))
    expert_ids_keys = jax.random.split(jax.random.fold_in(part_keys[1], 1), ROWS // ROW_DEV)
    expert_ids_turns = jax.random.permutation(jax.random.fold_in(part_keys[1], 3), ROWS // ROW_DEV)
    expert_ids = jax.vmap(lambda own, number: routed_block(jax.random.fold_in(part_keys[1], 2), own, number, ROW_DEV, EXPERTS, TOP, CAP, 2))(expert_ids_keys, expert_ids_turns).reshape((ROWS, TOP))
    gate_values = jnp.clip(0.1 + 0.9 * jax.random.uniform(part_keys[2], (ROWS, TOP), jnp.float32) ** levels(part_keys[2], (ROWS, TOP), ((0, 16),), -0.2, 0.2), 0.1, 1.0)
    expert_block = jax.random.permutation(streams_of[3], EXPERTS).astype(jnp.int32)
    w_gate = scatter_about(streams_of[4], (D, EXPERTS * FFE), D ** -0.5, 0.0625, ((1, 16),))
    w_up = scatter_about(streams_of[5], (D, EXPERTS * FFE), D ** -0.5, 0.0625, ((1, 16),))
    w_down = scatter_about(streams_of[6], (EXPERTS * FFE, D), FFE ** -0.5, 0.1875, ((0, 16),))
    return {"hidden_rows": hidden_rows, "expert_ids": expert_ids, "gate_values": gate_values, "expert_block": expert_block, "w_gate": w_gate, "w_up": w_up, "w_down": w_down}


def slot_numbers(block_ids, experts):
    flat_ids = block_ids.reshape(-1)
    onehot = (flat_ids[:, None] == jnp.arange(experts, dtype=jnp.int32)[None, :]).astype(jnp.int32)
    before = jnp.cumsum(onehot, axis=0) - onehot
    return jnp.sum(before * onehot, axis=1).astype(jnp.int32)


def reference(hidden_rows, expert_ids, gate_values, expert_block, w_gate, w_up, w_down):
    devices = N_NODE * N_LOCAL
    blocked = expert_ids.reshape(devices, ROW_DEV, TOP)
    slot_index = jax.vmap(lambda block_ids: slot_numbers(block_ids, EXPERTS))(blocked).reshape(-1)
    flat_ids = expert_ids.reshape(-1).astype(jnp.int32)
    source = jnp.arange(ROWS * TOP, dtype=jnp.int32) // (ROW_DEV * TOP)
    row_index = jnp.arange(ROWS * TOP, dtype=jnp.int32) // TOP
    position = (source * CAP + slot_index).astype(jnp.int32)
    buffers = jnp.zeros((EXPERTS, devices * CAP, D), jnp.bfloat16).at[flat_ids, position].set(hidden_rows[row_index])

    def one_expert(expert):
        col_start = (expert_block[expert] * FFE).astype(jnp.int32)
        gate_cols = lax.dynamic_slice_in_dim(w_gate, col_start, FFE, 1)
        up_cols = lax.dynamic_slice_in_dim(w_up, col_start, FFE, 1)
        down_rows = lax.dynamic_slice_in_dim(w_down, col_start, FFE, 0)
        inputs = buffers[expert]
        gate_act = jnp.dot(inputs, gate_cols, preferred_element_type=jnp.float32)
        up_act = jnp.dot(inputs, up_cols, preferred_element_type=jnp.float32)
        hidden = (jax.nn.silu(gate_act) * up_act).astype(jnp.bfloat16)
        total = jnp.zeros((devices * CAP, D), jnp.float32)
        for quarter in range(4):
            piece = jnp.dot(hidden[:, quarter * QUARTER:(quarter + 1) * QUARTER],
                            down_rows[quarter * QUARTER:(quarter + 1) * QUARTER],
                            preferred_element_type=jnp.float32).astype(jnp.bfloat16)
            piece = lax.optimization_barrier(piece)
            total = total + piece.astype(jnp.float32)
        return total.astype(jnp.bfloat16)

    outputs = lax.map(one_expert, jnp.arange(EXPERTS, dtype=jnp.int32))
    picked = outputs[flat_ids, position].astype(jnp.float32).reshape(ROWS, TOP, D)
    combined = jnp.sum(picked * gate_values[:, :, None], axis=1)
    return combined.astype(jnp.bfloat16)
```

```python
import functools
import jax
import jax.numpy as jnp
from jax import lax
from jax.experimental import pallas as pl
from jax.experimental.pallas import tpu as pltpu
from jax.sharding import PartitionSpec as P

MESH = pl.DeviceIdType.MESH
CHUNKS = 4


def routed_kernel(planes, ids_ref, gate_ref, block_ref, x_ref, wg_ref, wu_ref, wd_ref, out_ref,
                  w1, wd, xs, xr, cs, cr, rows_in, acc, ps, pr, ys, yr, keep, zs, zr, fs, fr,
                  w_sem, one_sem, chunk_send, chunk_recv, zin_send, zin_recv, zout_send, zout_recv):
    node, core = lax.axis_index("node"), lax.axis_index("local")
    plane, column = node // 2, node % 2
    row_count, width = x_ref.shape
    half = width // 2
    chunks = xs.shape[0]
    piece = half // chunks
    pair = 2 * row_count
    hidden_units = wg_ref.shape[1]
    other_core = 1 - core
    sibling = {"local": other_core}
    across = {"node": plane * 2 + (1 - column)}

    def plane_at(step):
        return {"node": lax.rem(plane + step, planes) * 2 + column}

    def start_of(rel, k):
        side = core if rel == 0 else other_core
        return pl.multiple_of(side * half + k * piece, 128)

    loads = {}
    for rel in range(2):
        for k in range(chunks):
            span = pl.ds(start_of(rel, k), piece)
            loads[0, rel, k] = pltpu.make_async_copy(
                wg_ref.at[span, :], w1.at[rel, k, :, pl.ds(0, hidden_units)], w_sem.at[0, rel, k])
            loads[1, rel, k] = pltpu.make_async_copy(
                wu_ref.at[span, :], w1.at[rel, k, :, pl.ds(hidden_units, hidden_units)], w_sem.at[1, rel, k])
            loads[2, rel, k] = pltpu.make_async_copy(wd_ref.at[:, span], wd.at[rel, k], w_sem.at[2, rel, k])
    for kind in ((0, 1), (2,)):
        for rel in range(2):
            for k in range(chunks):
                for which in kind:
                    loads[which, rel, k].start()

    barrier = pltpu.get_barrier_semaphore()
    partners = [sibling, across] + [plane_at(j) for j in range(1, planes)]
    for partner in partners:
        pl.semaphore_signal(barrier, inc=1, device_id=partner, device_id_type=MESH)

    for k in range(chunks):
        xs[k] = x_ref[:, pl.ds(start_of(1, k), piece)].astype(jnp.float32)
    ids = ids_ref[...]
    gates = gate_ref[...]
    target = jnp.zeros(ids.shape, jnp.int32)
    for e in range(block_ref.shape[0]):
        ahead = block_ref[e] - plane
        target = jnp.where(ids == e, jnp.where(ahead < 0, ahead + planes, ahead), target)
    lane = lax.broadcasted_iota(jnp.int32, cs.shape, 1)
    weight = jnp.zeros(cs.shape, jnp.float32)
    for k in range(ids.shape[1]):
        weight += jnp.where(target[:, k:k + 1] == lane, gates[:, k:k + 1], 0.0)
    cs[...] = weight

    pl.semaphore_wait(barrier, len(partners))

    sent = []

    def send(src, dst, send_sem, recv_sem, to):
        copy = pltpu.make_async_remote_copy(
            src_ref=src, dst_ref=dst, send_sem=send_sem, recv_sem=recv_sem, device_id=to, device_id_type=MESH)
        copy.start()
        sent.append(copy)
        return copy

    def by_chunk(kind, k, src, dst, to):
        return send(src, dst, chunk_send.at[kind, k], chunk_recv.at[kind, k], to)

    def in_order(own, other):
        return jnp.where(core == 0, jnp.concatenate([own, other], 0), jnp.concatenate([other, own], 0))

    swaps = [by_chunk(0, k, xs.at[k], xr.at[k], sibling) for k in range(chunks)]
    weights_swap = send(cs, cr, one_sem.at[0], one_sem.at[1], sibling)
    first, rest = pl.ds(0, pair), pl.ds(pair, (planes - 1) * pair)
    z_in, y_first, y_rest, b_first, b_rest, b_across = [], [], [], [], [], []
    for k in range(chunks):
        swaps[k].wait_recv()
        own = x_ref[:, pl.ds(start_of(0, k), piece)].astype(jnp.float32)
        rows_in[0, k, 0, first, :] = in_order(own, xr[k]).astype(jnp.bfloat16)
        mine = rows_in.at[0, k, 0, first, :]
        z_in.append([
            send(mine, rows_in.at[0, k, 0, pl.ds((planes - j) * pair, pair), :],
                 zin_send.at[k, planes - j], zin_recv.at[k, planes - j], plane_at(j))
            for j in range(1, planes)])
        y_first.append(by_chunk(1, k, mine, rows_in.at[0, k, 1, first, :], across))
        b_first.append(by_chunk(2, k, mine, rows_in.at[1, k, 0, first, :], sibling))

    acc[...] = jnp.zeros_like(acc)

    def pass_on(k):
        for copy in z_in[k]:
            copy.wait_recv()
        came = rows_in.at[0, k, 0, rest, :]
        y_rest.append(by_chunk(3, k, came, rows_in.at[0, k, 1, rest, :], across))
        b_rest.append(by_chunk(4, k, came, rows_in.at[1, k, 0, rest, :], sibling))

    def multiply(rel, k):
        loads[0, rel, k].wait()
        loads[1, rel, k].wait()
        lhs = rows_in[rel, k].reshape(2 * planes * pair, piece)
        acc[...] += jnp.dot(lhs, w1[rel, k], preferred_element_type=jnp.float32)

    def take_across(k):
        y_first[k].wait_recv()
        y_rest[k].wait_recv()
        b_across.append(by_chunk(5, k, rows_in.at[0, k, 1], rows_in.at[1, k, 1], sibling))
        multiply(0, k)

    def take_sibling(k):
        b_first[k].wait_recv()
        b_rest[k].wait_recv()
        b_across[k].wait_recv()
        multiply(1, k)

    for k in range(chunks + 2):
        if k < chunks:
            pass_on(k)
        if 1 <= k <= chunks:
            take_across(k - 1)
        if k >= 2:
            take_sibling(k - 2)

    gate_act = acc[:, :hidden_units]
    hidden = (gate_act / (1.0 + jnp.exp(-gate_act)) * acc[:, hidden_units:]).astype(jnp.bfloat16)
    weights_swap.wait_recv()
    weight = in_order(weight, cr[...])

    def part(rel, k):
        loads[2, rel, k].wait()
        return jnp.dot(hidden, wd[rel, k], preferred_element_type=jnp.float32)

    p_out, y_out, z_out, f_out = [], [], [], []

    def stage_a(k):
        ps[k] = part(1, k).astype(jnp.bfloat16)
        p_out.append(by_chunk(6, k, ps.at[k], pr.at[k], sibling))

    def stage_b(k):
        mine = part(0, k)
        p_out[k].wait_recv()
        total = mine + pr[k].astype(jnp.float32)
        ys[k] = total[planes * pair:].astype(jnp.bfloat16)
        y_out.append(by_chunk(7, k, ys.at[k], yr.at[k], across))
        keep[k] = total[:planes * pair]

    def stage_c(k):
        y_out[k].wait_recv()
        zs[k] = (keep[k] + yr[k].astype(jnp.float32)).astype(jnp.bfloat16)
        z_out.append([
            send(zs.at[k, pl.ds(j * pair, pair), :], zr.at[k, pl.ds((planes - j) * pair, pair), :],
                 zout_send.at[k, planes - j], zout_recv.at[k, planes - j], plane_at(j))
            for j in range(1, planes)])

    def stage_d(k):
        for copy in z_out[k]:
            copy.wait_recv()
        total = weight[:, 0:1] * zs[k, first, :].astype(jnp.float32)
        for s in range(1, planes):
            total += weight[:, s:s + 1] * zr[k, pl.ds(s * pair, pair), :].astype(jnp.float32)
        low, high = total[:row_count], total[row_count:]
        fs[k] = jnp.where(core == 0, high, low)
        f_out.append(by_chunk(8, k, fs.at[k], fr.at[k], sibling))
        out_ref[:, pl.ds(start_of(0, k), piece)] = jnp.where(core == 0, low, high)

    stage_a(0)
    for k in range(chunks):
        if k + 1 < chunks:
            stage_a(k + 1)
        stage_b(k)
    for k in range(chunks + 1):
        if k < chunks:
            stage_c(k)
        if k >= 1:
            stage_d(k - 1)
    for k in range(chunks):
        f_out[k].wait_recv()
        out_ref[:, pl.ds(start_of(1, k), piece)] = fr[k]
    for copy in sent:
        copy.wait_send()


def per_device(hidden_rows, expert_ids, gate_values, expert_block, w_gate, w_up, w_down):
    rows, width = hidden_rows.shape
    planes = lax.axis_size("node") // 2
    units = w_gate.shape[1]
    pair, chunks = 2 * rows, CHUNKS
    piece = width // 2 // chunks
    column = planes * pair
    bf16, f32 = jnp.bfloat16, jnp.float32
    vmem = pl.BlockSpec(memory_space=pltpu.VMEM)
    anywhere = pl.BlockSpec(memory_space=pl.ANY)
    dma = pltpu.SemaphoreType.DMA
    combined = pl.pallas_call(
        functools.partial(routed_kernel, planes),
        out_shape=jax.ShapeDtypeStruct((rows, width), f32),
        in_specs=[vmem, vmem, pl.BlockSpec(memory_space=pltpu.SMEM), vmem, anywhere, anywhere, anywhere],
        out_specs=vmem,
        scratch_shapes=[
            pltpu.VMEM((2, chunks, piece, 2 * units), bf16),
            pltpu.VMEM((2, chunks, units, piece), bf16),
            pltpu.VMEM((chunks, rows, piece), f32),
            pltpu.VMEM((chunks, rows, piece), f32),
            pltpu.VMEM((rows, 128), f32),
            pltpu.VMEM((rows, 128), f32),
            pltpu.VMEM((2, chunks, 2, column, piece), bf16),
            pltpu.VMEM((2 * column, 2 * units), f32),
            pltpu.VMEM((chunks, 2 * column, piece), bf16),
            pltpu.VMEM((chunks, 2 * column, piece), bf16),
            pltpu.VMEM((chunks, column, piece), bf16),
            pltpu.VMEM((chunks, column, piece), bf16),
            pltpu.VMEM((chunks, column, piece), f32),
            pltpu.VMEM((chunks, column, piece), bf16),
            pltpu.VMEM((chunks, column, piece), bf16),
            pltpu.VMEM((chunks, rows, piece), f32),
            pltpu.VMEM((chunks, rows, piece), f32),
            dma((3, 2, chunks)),
            dma((2,)),
            dma((9, chunks)),
            dma((9, chunks)),
            dma((chunks, planes)),
            dma((chunks, planes)),
            dma((chunks, planes)),
            dma((chunks, planes)),
        ],
        compiler_params=pltpu.CompilerParams(
            collective_id=0, has_side_effects=True, vmem_limit_bytes=56 * 1024 * 1024),
    )(expert_ids, gate_values, expert_block, hidden_rows, w_gate, w_up, w_down)
    return combined.astype(bf16)


def solution(mesh):
    placed = (
        P(("groups", "node", "local"), None),
        P(("groups", "node", "local"), None),
        P(("groups", "node", "local"), None),
        P(),
        P(None, ("node", "local")),
        P(None, ("node", "local")),
        P(("node", "local"), None),
    )
    return jax.shard_map(
        per_device,
        mesh=mesh,
        in_specs=placed,
        out_specs=P(("groups", "node", "local"), None),
        check_vma=False,
    )
```

```python
import functools
import jax
import jax.numpy as jnp
from jax import lax
from jax.experimental import pallas as pl
from jax.experimental.pallas import tpu as pltpu
from jax.sharding import PartitionSpec as P

MESH = pl.DeviceIdType.MESH
CHUNKS = 4


def routed_kernel(planes, ids_ref, gate_ref, block_ref, x_ref, wg_ref, wu_ref, wd_ref, out_ref,
                  w1, wd, rows_in, acc, mine, ps, pr, ys, yr, keep, zs, zr,
                  w_sem, chunk_send, chunk_recv, zin_send, zin_recv, zout_send, zout_recv):
    node, core = lax.axis_index("node"), lax.axis_index("local")
    plane, column = node // 2, node % 2
    row_count, width = x_ref.shape
    half = width // 2
    chunks = ps.shape[0]
    piece = half // chunks
    pair = 2 * row_count
    hidden_units = wg_ref.shape[1]
    sibling = {"local": 1 - core}
    across = {"node": plane * 2 + (1 - column)}

    def plane_at(step):
        return {"node": lax.rem(plane + step, planes) * 2 + column}

    def span(side, k):
        return pl.ds(side * half + k * piece, piece)

    barrier = pltpu.get_barrier_semaphore()
    partners = [sibling, across] + [plane_at(j) for j in range(1, planes)]
    for partner in partners:
        pl.semaphore_signal(barrier, inc=1, device_id=partner, device_id_type=MESH)

    first, rest = pl.ds(0, pair), pl.ds(pair, (planes - 1) * pair)
    for k in range(chunks):
        packed = jnp.concatenate([x_ref[:, span(0, k)].astype(jnp.float32), x_ref[:, span(1, k)].astype(jnp.float32)], 0)
        rows_in[0, k, 0, first, :] = packed.astype(jnp.bfloat16)

    pl.semaphore_wait(barrier, len(partners))

    sent = []

    def send(src, dst, send_sem, recv_sem, to):
        copy = pltpu.make_async_remote_copy(
            src_ref=src, dst_ref=dst, send_sem=send_sem, recv_sem=recv_sem, device_id=to, device_id_type=MESH)
        copy.start()
        sent.append(copy)
        return copy

    def by_chunk(kind, k, src, dst, to):
        return send(src, dst, chunk_send.at[kind, k], chunk_recv.at[kind, k], to)

    z_in, y_first, y_rest, b_first, b_rest, b_across = [], [], [], [], [], []
    for k in range(chunks):
        own = rows_in.at[0, k, 0, first, :]
        z_in.append([
            send(own, rows_in.at[0, k, 0, pl.ds((planes - j) * pair, pair), :],
                 zin_send.at[k, planes - j], zin_recv.at[k, planes - j], plane_at(j))
            for j in range(1, planes)])
        y_first.append(by_chunk(1, k, own, rows_in.at[0, k, 1, first, :], across))
        b_first.append(by_chunk(2, k, own, rows_in.at[1, k, 0, first, :], sibling))

    loads = {}
    for side in range(2):
        for k in range(chunks):
            loads[0, side, k] = pltpu.make_async_copy(
                wg_ref.at[span(side, k), :], w1.at[side, k, :, pl.ds(0, hidden_units)], w_sem.at[0, side, k])
            loads[1, side, k] = pltpu.make_async_copy(
                wu_ref.at[span(side, k), :], w1.at[side, k, :, pl.ds(hidden_units, hidden_units)], w_sem.at[1, side, k])
            loads[2, side, k] = pltpu.make_async_copy(wd_ref.at[:, span(side, k)], wd.at[side, k], w_sem.at[2, side, k])
    for kinds in ((0, 1), (2,)):
        for k in range(chunks):
            for side in range(2):
                for kind in kinds:
                    loads[kind, side, k].start()

    ids = ids_ref[...]
    gates = gate_ref[...]
    target = jnp.zeros(ids.shape, jnp.int32)
    for e in range(block_ref.shape[0]):
        ahead = block_ref[e] - plane
        target = jnp.where(ids == e, jnp.where(ahead < 0, ahead + planes, ahead), target)
    square = (row_count, row_count)
    diagonal = lax.broadcasted_iota(jnp.int32, square, 0) == lax.broadcasted_iota(jnp.int32, square, 1)
    weights = []
    for s in range(planes):
        line = jnp.sum(jnp.where(target == s, gates, 0.0), axis=0, keepdims=True)
        upright = jnp.sum(jnp.where(diagonal, jnp.broadcast_to(line, square), 0.0), axis=1, keepdims=True)
        weights.append(jnp.concatenate([upright, upright], 0))

    acc[...] = jnp.zeros_like(acc)

    def pass_on(k):
        for copy in z_in[k]:
            copy.wait_recv()
        came = rows_in.at[0, k, 0, rest, :]
        y_rest.append(by_chunk(3, k, came, rows_in.at[0, k, 1, rest, :], across))
        b_rest.append(by_chunk(4, k, came, rows_in.at[1, k, 0, rest, :], sibling))

    def take_across(k):
        y_first[k].wait_recv()
        y_rest[k].wait_recv()
        b_across.append(by_chunk(5, k, rows_in.at[0, k, 1], rows_in.at[1, k, 1], sibling))

    def multiply(k):
        b_first[k].wait_recv()
        b_rest[k].wait_recv()
        b_across[k].wait_recv()
        loose = []
        for c in range(2):
            loose.append(rows_in[c, k].reshape(2 * planes, pair, piece).astype(jnp.float32))
        for side in range(2):
            loads[0, side, k].wait()
            loads[1, side, k].wait()
            lhs = jnp.concatenate([
                part[:, side * row_count:(side + 1) * row_count].reshape(planes * pair, piece) for part in loose], 0)
            acc[...] += jnp.dot(lhs.astype(jnp.bfloat16), w1[side, k], preferred_element_type=jnp.float32)

    for k in range(chunks + 2):
        if k < chunks:
            pass_on(k)
        if 1 <= k <= chunks:
            take_across(k - 1)
        if k >= 2:
            multiply(k - 2)

    gate_act = acc[:, :hidden_units]
    hidden = (gate_act / (1.0 + jnp.exp(-gate_act)) * acc[:, hidden_units:]).astype(jnp.bfloat16)

    p_out, y_out, z_out = [], [], []
    groups = 4 * planes

    def stage_a(k):
        sides = []
        for side in range(2):
            loads[2, side, k].wait()
            product = jnp.dot(hidden, wd[side, k], preferred_element_type=jnp.float32)
            sides.append(product.reshape(groups, row_count, piece))
        both = jnp.concatenate(sides, 1).reshape(groups * pair, piece)
        ps[k] = both[groups // 2 * pair:].astype(jnp.bfloat16)
        p_out.append(by_chunk(6, k, ps.at[k], pr.at[k], sibling))
        mine[k] = both[:groups // 2 * pair]

    def stage_b(k):
        p_out[k].wait_recv()
        total = mine[k] + pr[k].astype(jnp.float32)
        ys[k] = total[planes * pair:].astype(jnp.bfloat16)
        y_out.append(by_chunk(7, k, ys.at[k], yr.at[k], across))
        keep[k] = total[:planes * pair]

    def stage_c(k):
        y_out[k].wait_recv()
        zs[k] = (keep[k] + yr[k].astype(jnp.float32)).astype(jnp.bfloat16)
        z_out.append([
            send(zs.at[k, pl.ds(j * pair, pair), :], zr.at[k, pl.ds((planes - j) * pair, pair), :],
                 zout_send.at[k, planes - j], zout_recv.at[k, planes - j], plane_at(j))
            for j in range(1, planes)])

    def stage_d(k):
        for copy in z_out[k]:
            copy.wait_recv()
        total = weights[0] * zs[k, first, :].astype(jnp.float32)
        for s in range(1, planes):
            total += weights[s] * zr[k, pl.ds(s * pair, pair), :].astype(jnp.float32)
        out_ref[:, span(0, k)] = total[:row_count]
        out_ref[:, span(1, k)] = total[row_count:]

    stage_a(0)
    stage_a(1)
    for k in range(chunks):
        if k + 2 < chunks:
            stage_a(k + 2)
        stage_b(k)
    for k in range(chunks + 2):
        if k < chunks:
            stage_c(k)
        if k >= 2:
            stage_d(k - 2)
    for copy in sent:
        copy.wait_send()


def per_device(hidden_rows, expert_ids, gate_values, expert_block, w_gate, w_up, w_down):
    rows, width = hidden_rows.shape
    planes = lax.axis_size("node") // 2
    units = w_gate.shape[1]
    pair, chunks = 2 * rows, CHUNKS
    piece = width // 2 // chunks
    column = planes * pair
    bf16, f32 = jnp.bfloat16, jnp.float32
    vmem = pl.BlockSpec(memory_space=pltpu.VMEM)
    anywhere = pl.BlockSpec(memory_space=pl.ANY)
    dma = pltpu.SemaphoreType.DMA
    combined = pl.pallas_call(
        functools.partial(routed_kernel, planes),
        out_shape=jax.ShapeDtypeStruct((rows, width), f32),
        in_specs=[vmem, vmem, pl.BlockSpec(memory_space=pltpu.SMEM), vmem, anywhere, anywhere, anywhere],
        out_specs=vmem,
        scratch_shapes=[
            pltpu.VMEM((2, chunks, piece, 2 * units), bf16),
            pltpu.VMEM((2, chunks, units, piece), bf16),
            pltpu.VMEM((2, chunks, 2, column, piece), bf16),
            pltpu.VMEM((2 * column, 2 * units), f32),
            pltpu.VMEM((chunks, 2 * column, piece), f32),
            pltpu.VMEM((chunks, 2 * column, piece), bf16),
            pltpu.VMEM((chunks, 2 * column, piece), bf16),
            pltpu.VMEM((chunks, column, piece), bf16),
            pltpu.VMEM((chunks, column, piece), bf16),
            pltpu.VMEM((chunks, column, piece), f32),
            pltpu.VMEM((chunks, column, piece), bf16),
            pltpu.VMEM((chunks, column, piece), bf16),
            dma((3, 2, chunks)),
            dma((8, chunks)),
            dma((8, chunks)),
            dma((chunks, planes)),
            dma((chunks, planes)),
            dma((chunks, planes)),
            dma((chunks, planes)),
        ],
        compiler_params=pltpu.CompilerParams(
            collective_id=0, has_side_effects=True, vmem_limit_bytes=56 * 1024 * 1024),
    )(expert_ids.T, gate_values.T, expert_block, hidden_rows, w_gate, w_up, w_down)
    return combined.astype(bf16)


def solution(mesh):
    placed = (
        P(("groups", "node", "local"), None),
        P(("groups", "node", "local"), None),
        P(("groups", "node", "local"), None),
        P(),
        P(None, ("node", "local")),
        P(None, ("node", "local")),
        P(("node", "local"), None),
    )
    return jax.shard_map(
        per_device,
        mesh=mesh,
        in_specs=placed,
        out_specs=P(("groups", "node", "local"), None),
        check_vma=False,
    )
```

```python
import functools
import jax
import jax.numpy as jnp
from jax import lax
from jax.experimental import pallas as pl
from jax.experimental.pallas import tpu as pltpu
from jax.sharding import PartitionSpec as P

MESH = pl.DeviceIdType.MESH
PIECES = 8


def lane_spans(piece):
    cut = -(-piece // 256) * 128
    return [(0, cut), (cut, piece - cut)]


def routed_kernel(planes, capacity, ids_ref, gate_ref, block_ref, x_ref, wg_ref, wu_ref, wd_ref, out_ref,
                  w1, wd, xsend, rows_in, loose, acc, product, ps, pr, ys, yr, keep, zs, zr,
                  w_sem, chunk_send, chunk_recv, zin_send, zin_recv, zout_send, zout_recv):
    node, core = lax.axis_index("node"), lax.axis_index("local")
    plane, column = node // 2, node % 2
    row_count, width = x_ref.shape
    piece = width // PIECES
    spans = lane_spans(piece)
    chunks = len(spans)
    pair = capacity * PIECES
    column_rows = planes * pair
    hidden_units = wg_ref.shape[1]
    f32, bf16 = jnp.float32, jnp.bfloat16
    sibling = {"local": 1 - core}
    across = {"node": plane * 2 + (1 - column)}

    def plane_at(step):
        return {"node": lax.rem(plane + step, planes) * 2 + column}

    def lanes(k):
        return pl.ds(*spans[k])

    def at_piece(p, k):
        return pl.ds(p * piece + spans[k][0], spans[k][1])

    barrier = pltpu.get_barrier_semaphore()
    partners = [sibling, across] + [plane_at(j) for j in range(1, planes)]
    for partner in partners:
        pl.semaphore_signal(barrier, inc=1, device_id=partner, device_id_type=MESH)

    first, rest = pl.ds(0, pair), pl.ds(pair, (planes - 1) * pair)

    loads = {}
    for k in range(chunks):
        for p in range(PIECES):
            here = at_piece(p, k)
            loads[0, p, k] = pltpu.make_async_copy(
                wg_ref.at[here, :], w1.at[here, pl.ds(0, hidden_units)], w_sem.at[0, p, k])
            loads[1, p, k] = pltpu.make_async_copy(
                wu_ref.at[here, :], w1.at[here, pl.ds(hidden_units, hidden_units)], w_sem.at[1, p, k])
            loads[2, p, k] = pltpu.make_async_copy(wd_ref.at[:, here], wd.at[:, here], w_sem.at[2, p, k])
            loads[0, p, k].start()
            loads[1, p, k].start()
    for k in range(chunks):
        for p in range(PIECES):
            loads[2, p, k].start()

    def iota(shape, dim):
        return lax.broadcasted_iota(jnp.int32, shape, dim)

    def exact_dot(a, b):
        return jnp.dot(a.astype(f32).astype(bf16), b.astype(f32).astype(bf16), preferred_element_type=f32)

    ids = ids_ref[...]
    gates = gate_ref[...]
    target = jnp.zeros(ids.shape, jnp.int32)
    for e in range(block_ref.shape[0]):
        ahead = block_ref[e] - plane
        target = jnp.where(ids == e, jnp.where(ahead < 0, ahead + planes, ahead), target)
    table = (planes, row_count)
    named = jnp.zeros(table, f32)
    for c in range(ids.shape[0]):
        named += jnp.where(jnp.broadcast_to(target[c:c + 1], table) == iota(table, 0), 1.0, 0.0)
    square = (row_count, row_count)
    before = exact_dot(named, jnp.where(iota(square, 0) < iota(square, 1), 1.0, 0.0))
    place = jnp.where(named > 0.5, before + (capacity * iota(table, 0)).astype(f32), 250.0)
    spread = (planes * capacity, planes)
    offset = iota(spread, 0) - capacity * iota(spread, 1)
    expand = jnp.where((offset >= 0) & (offset < capacity), 1.0, 0.0)
    grid = (planes * capacity, row_count)
    hits = jnp.where(exact_dot(expand, place) == iota(grid, 0).astype(f32), 1.0, 0.0)
    wide = (row_count, PIECES * row_count)
    hits = exact_dot(hits, jnp.where(iota(wide, 1) % row_count == iota(wide, 0), 1.0, 0.0))
    tall = (column_rows, planes * capacity)
    hits = exact_dot(jnp.where(iota(tall, 0) // PIECES == iota(tall, 1), 1.0, 0.0), hits)
    full = (column_rows, PIECES * row_count)
    choose = jnp.where(iota(full, 0) % PIECES == iota(full, 1) // row_count, hits, 0.0).astype(bf16)

    first, rest = pl.ds(0, pair), pl.ds(pair, column_rows - pair)
    for k in range(chunks):
        packed = jnp.concatenate([x_ref[:, at_piece(p, k)].astype(f32) for p in range(PIECES)], 0).astype(bf16)
        chosen = jnp.dot(choose, packed, preferred_element_type=f32).astype(bf16)
        xsend[:, lanes(k)] = chosen
        rows_in[0, 0, first, lanes(k)] = chosen[:pair]

    pl.semaphore_wait(barrier, len(partners))

    sent = []

    def send(src, dst, send_sem, recv_sem, to):
        copy = pltpu.make_async_remote_copy(
            src_ref=src, dst_ref=dst, send_sem=send_sem, recv_sem=recv_sem, device_id=to, device_id_type=MESH)
        copy.start()
        sent.append(copy)
        return copy

    def by_chunk(kind, k, src, dst, to):
        return send(src, dst, chunk_send.at[kind, k], chunk_recv.at[kind, k], to)

    z_in, y_first, y_rest, b_first, b_rest, b_across = [], [], [], [], [], []
    for k in range(chunks):
        z_in.append([
            send(xsend.at[pl.ds(j * pair, pair), lanes(k)],
                 rows_in.at[0, 0, pl.ds((planes - j) * pair, pair), lanes(k)],
                 zin_send.at[k, planes - j], zin_recv.at[k, planes - j], plane_at(j))
            for j in range(1, planes)])
        own = rows_in.at[0, 0, first, lanes(k)]
        y_first.append(by_chunk(1, k, own, rows_in.at[0, 1, first, lanes(k)], across))
        b_first.append(by_chunk(2, k, own, rows_in.at[1, 0, first, lanes(k)], sibling))

    diagonal = iota(square, 0) == iota(square, 1)
    weights = []
    for s in range(planes):
        line = jnp.sum(jnp.where(target == s, gates, 0.0), axis=0, keepdims=True)
        upright = jnp.sum(jnp.where(diagonal, jnp.broadcast_to(line, square), 0.0), axis=1, keepdims=True)
        weights.append(jnp.concatenate([upright] * PIECES, 0))

    acc[...] = jnp.zeros_like(acc)
    block_rows = 4 * planes * capacity

    def pass_on(k):
        for copy in z_in[k]:
            copy.wait_recv()
        came = rows_in.at[0, 0, rest, lanes(k)]
        y_rest.append(by_chunk(3, k, came, rows_in.at[0, 1, rest, lanes(k)], across))
        b_rest.append(by_chunk(4, k, came, rows_in.at[1, 0, rest, lanes(k)], sibling))

    def take_across(k):
        y_first[k].wait_recv()
        y_rest[k].wait_recv()
        b_across.append(by_chunk(5, k, rows_in.at[0, 1, :, lanes(k)], rows_in.at[1, 1, :, lanes(k)], sibling))

    def multiply(k):
        b_first[k].wait_recv()
        b_rest[k].wait_recv()
        b_across[k].wait_recv()
        start, size = spans[k]
        for t in range(size // 128):
            tile = rows_in[:, :, :, pl.ds(start + t * 128, 128)]
            loose[t] = tile.reshape(4 * column_rows, 128).astype(f32)
        for p in range(PIECES):
            loads[0, p, k].wait()
            loads[1, p, k].wait()
            lhs = jnp.concatenate([
                loose[t, pl.ds(p, block_rows, stride=PIECES), :] for t in range(size // 128)], 1)
            acc[...] += jnp.dot(lhs.astype(bf16), w1[at_piece(p, k), :], preferred_element_type=f32)

    for k in range(chunks):
        pass_on(k)
        if k >= 1:
            take_across(k - 1)
    take_across(chunks - 1)
    for k in range(chunks):
        multiply(k)

    gate_act = acc[:, :hidden_units]
    hidden = (gate_act / (1.0 + jnp.exp(-gate_act)) * acc[:, hidden_units:]).astype(bf16)

    p_out, y_out, z_out = [], [], []

    def stage_a(k):
        start, size = spans[k]
        for p in range(PIECES):
            loads[2, p, k].wait()
            result = jnp.dot(hidden, wd[:, at_piece(p, k)], preferred_element_type=f32)
            for t in range(size // 128):
                product[start // 128 + t, pl.ds(p, block_rows, stride=PIECES), :] = result[:, t * 128:(t + 1) * 128]
        for t in range(size // 128):
            ps[:, pl.ds(start + t * 128, 128)] = product[
                start // 128 + t, pl.ds(2 * column_rows, 2 * column_rows), :].astype(bf16)
        p_out.append(by_chunk(6, k, ps.at[:, lanes(k)], pr.at[:, lanes(k)], sibling))

    def stage_b(k):
        p_out[k].wait_recv()
        start, size = spans[k]
        for t in range(size // 128):
            here = pl.ds(start + t * 128, 128)
            total = product[start // 128 + t, pl.ds(0, 2 * column_rows), :] + pr[:, here].astype(f32)
            ys[:, here] = total[column_rows:].astype(bf16)
            keep[:, here] = total[:column_rows]
        y_out.append(by_chunk(7, k, ys.at[:, lanes(k)], yr.at[:, lanes(k)], across))

    def stage_c(k):
        y_out[k].wait_recv()
        zs[:, lanes(k)] = (keep[:, lanes(k)] + yr[:, lanes(k)].astype(f32)).astype(bf16)
        z_out.append([
            send(zs.at[pl.ds(j * pair, pair), lanes(k)], zr.at[pl.ds((planes - j) * pair, pair), lanes(k)],
                 zout_send.at[k, planes - j], zout_recv.at[k, planes - j], plane_at(j))
            for j in range(1, planes)])

    def stage_d(k):
        for copy in z_out[k]:
            copy.wait_recv()
        total = None
        for s in range(planes):
            block = zs[first, lanes(k)] if s == 0 else zr[pl.ds(s * pair, pair), lanes(k)]
            picked = lax.dot_general(
                choose[s * pair:(s + 1) * pair], block, (((0,), (0,)), ((), ())), preferred_element_type=f32)
            total = weights[s] * picked if s == 0 else total + weights[s] * picked
        for p in range(PIECES):
            out_ref[:, at_piece(p, k)] = total[p * row_count:(p + 1) * row_count]

    for k in range(chunks):
        stage_a(k)
        if k >= 1:
            stage_b(k - 1)
    stage_b(chunks - 1)
    for k in range(chunks):
        stage_c(k)
    for k in range(chunks):
        stage_d(k)
    for copy in sent:
        copy.wait_send()


def per_device(hidden_rows, expert_ids, gate_values, expert_block, w_gate, w_up, w_down):
    rows, width = hidden_rows.shape
    planes = lax.axis_size("node") // 2
    units = w_gate.shape[1]
    capacity = rows * expert_ids.shape[1] * 3 // (2 * expert_block.shape[0])
    pair = capacity * PIECES
    piece = width // PIECES
    chunks = len(lane_spans(piece))
    largest = max(size for _, size in lane_spans(piece))
    column = planes * pair
    bf16, f32 = jnp.bfloat16, jnp.float32
    vmem = pl.BlockSpec(memory_space=pltpu.VMEM)
    anywhere = pl.BlockSpec(memory_space=pl.ANY)
    dma = pltpu.SemaphoreType.DMA
    combined = pl.pallas_call(
        functools.partial(routed_kernel, planes, capacity),
        out_shape=jax.ShapeDtypeStruct((rows, width), f32),
        in_specs=[vmem, vmem, pl.BlockSpec(memory_space=pltpu.SMEM), vmem, anywhere, anywhere, anywhere],
        out_specs=vmem,
        scratch_shapes=[
            pltpu.VMEM((width, 2 * units), bf16),
            pltpu.VMEM((units, width), bf16),
            pltpu.VMEM((column, piece), bf16),
            pltpu.VMEM((2, 2, column, piece), bf16),
            pltpu.VMEM((largest // 128, 4 * column, 128), f32),
            pltpu.VMEM((4 * planes * capacity, 2 * units), f32),
            pltpu.VMEM((piece // 128, 4 * column, 128), f32),
            pltpu.VMEM((2 * column, piece), bf16),
            pltpu.VMEM((2 * column, piece), bf16),
            pltpu.VMEM((column, piece), bf16),
            pltpu.VMEM((column, piece), bf16),
            pltpu.VMEM((column, piece), f32),
            pltpu.VMEM((column, piece), bf16),
            pltpu.VMEM((column, piece), bf16),
            dma((3, PIECES, chunks)),
            dma((8, chunks)),
            dma((8, chunks)),
            dma((chunks, planes)),
            dma((chunks, planes)),
            dma((chunks, planes)),
            dma((chunks, planes)),
        ],
        compiler_params=pltpu.CompilerParams(
            collective_id=0, has_side_effects=True, vmem_limit_bytes=56 * 1024 * 1024),
    )(expert_ids.T, gate_values.T, expert_block, hidden_rows, w_gate, w_up, w_down)
    return combined.astype(bf16)


def solution(mesh):
    placed = (
        P(("groups", "node", "local"), None),
        P(("groups", "node", "local"), None),
        P(("groups", "node", "local"), None),
        P(),
        P(None, ("node", "local")),
        P(None, ("node", "local")),
        P(("node", "local"), None),
    )
    return jax.shard_map(
        per_device,
        mesh=mesh,
        in_specs=placed,
        out_specs=P(("groups", "node", "local"), None),
        check_vma=False,
    )
```

```python
import functools
import jax
import jax.numpy as jnp
from jax import lax
from jax.experimental import pallas as pl
from jax.experimental.pallas import tpu as pltpu
from jax.sharding import PartitionSpec as P

MESH = pl.DeviceIdType.MESH
PIECES = 8


def lane_spans(piece):
    cut = piece // 256 * 128
    return [(0, cut), (cut, piece - cut)]


def routed_kernel(planes, capacity, ids_ref, gate_ref, block_ref, x_ref, wg_ref, wu_ref, wd_ref, out_ref,
                  w1, wd, xsend, rows_in, loose, acc, product, ps, pr, ys, yr, keep, zs, zr,
                  w_sem, chunk_send, chunk_recv, zin_send, zin_recv, zout_send, zout_recv):
    node, core = lax.axis_index("node"), lax.axis_index("local")
    plane, column = node // 2, node % 2
    row_count, width = x_ref.shape
    piece = width // PIECES
    spans = lane_spans(piece)
    chunks = len(spans)
    pair = capacity * PIECES
    column_rows = planes * pair
    hidden_units = wg_ref.shape[1]
    f32, bf16 = jnp.float32, jnp.bfloat16
    sibling = {"local": 1 - core}
    across = {"node": plane * 2 + (1 - column)}

    def plane_at(step):
        return {"node": lax.rem(plane + step, planes) * 2 + column}

    def lanes(k):
        return pl.ds(*spans[k])

    def at_piece(p, k):
        return pl.ds(p * piece + spans[k][0], spans[k][1])

    barrier = pltpu.get_barrier_semaphore()
    partners = [sibling, across] + [plane_at(j) for j in range(1, planes)]
    for partner in partners:
        pl.semaphore_signal(barrier, inc=1, device_id=partner, device_id_type=MESH)

    first, rest = pl.ds(0, pair), pl.ds(pair, (planes - 1) * pair)

    loads = [
        pltpu.make_async_copy(wg_ref, w1.at[:, pl.ds(0, hidden_units)], w_sem.at[0]),
        pltpu.make_async_copy(wu_ref, w1.at[:, pl.ds(hidden_units, hidden_units)], w_sem.at[1]),
        pltpu.make_async_copy(wd_ref, wd, w_sem.at[2])]
    for load in loads:
        load.start()

    def iota(shape, dim):
        return lax.broadcasted_iota(jnp.int32, shape, dim)

    def exact_dot(a, b):
        return jnp.dot(a.astype(f32).astype(bf16), b.astype(f32).astype(bf16), preferred_element_type=f32)

    ids = ids_ref[...]
    gates = gate_ref[...]
    target = jnp.zeros(ids.shape, jnp.int32)
    for e in range(block_ref.shape[0]):
        ahead = block_ref[e] - plane
        target = jnp.where(ids == e, jnp.where(ahead < 0, ahead + planes, ahead), target)
    table = (planes, row_count)
    named = jnp.zeros(table, f32)
    for c in range(ids.shape[0]):
        named += jnp.where(jnp.broadcast_to(target[c:c + 1], table) == iota(table, 0), 1.0, 0.0)
    square = (row_count, row_count)
    before = exact_dot(named, jnp.where(iota(square, 0) < iota(square, 1), 1.0, 0.0))
    place = jnp.where(named > 0.5, before + (capacity * iota(table, 0)).astype(f32), 250.0)
    spread = (planes * capacity, planes)
    offset = iota(spread, 0) - capacity * iota(spread, 1)
    expand = jnp.where((offset >= 0) & (offset < capacity), 1.0, 0.0)
    grid = (planes * capacity, row_count)
    hits = jnp.where(exact_dot(expand, place) == iota(grid, 0).astype(f32), 1.0, 0.0)
    wide = (row_count, PIECES * row_count)
    hits = exact_dot(hits, jnp.where(iota(wide, 1) % row_count == iota(wide, 0), 1.0, 0.0))
    tall = (column_rows, planes * capacity)
    hits = exact_dot(jnp.where(iota(tall, 0) // PIECES == iota(tall, 1), 1.0, 0.0), hits)
    full = (column_rows, PIECES * row_count)
    choose = jnp.where(iota(full, 0) % PIECES == iota(full, 1) // row_count, hits, 0.0).astype(bf16)

    first, rest = pl.ds(0, pair), pl.ds(pair, column_rows - pair)
    for k in range(chunks):
        packed = jnp.concatenate([x_ref[:, at_piece(p, k)].astype(f32) for p in range(PIECES)], 0).astype(bf16)
        chosen = jnp.dot(choose, packed, preferred_element_type=f32).astype(bf16)
        xsend[:, lanes(k)] = chosen
        rows_in[0, 0, first, lanes(k)] = chosen[:pair]

    pl.semaphore_wait(barrier, len(partners))

    sent = []

    def send(src, dst, send_sem, recv_sem, to):
        copy = pltpu.make_async_remote_copy(
            src_ref=src, dst_ref=dst, send_sem=send_sem, recv_sem=recv_sem, device_id=to, device_id_type=MESH)
        copy.start()
        sent.append(copy)
        return copy

    def by_chunk(kind, k, src, dst, to):
        return send(src, dst, chunk_send.at[kind, k], chunk_recv.at[kind, k], to)

    z_in, y_first, y_rest, b_rest, b_across = [], [], [], [], []
    for k in range(chunks):
        z_in.append([
            send(xsend.at[pl.ds(j * pair, pair), lanes(k)],
                 rows_in.at[0, 0, pl.ds((planes - j) * pair, pair), lanes(k)],
                 zin_send.at[k, planes - j], zin_recv.at[k, planes - j], plane_at(j))
            for j in range(1, planes)])
        own = rows_in.at[0, 0, first, lanes(k)]
        y_first.append(by_chunk(1, k, own, rows_in.at[0, 1, first, lanes(k)], across))

    diagonal = iota(square, 0) == iota(square, 1)
    weights = []
    for s in range(planes):
        line = jnp.sum(jnp.where(target == s, gates, 0.0), axis=0, keepdims=True)
        upright = jnp.sum(jnp.where(diagonal, jnp.broadcast_to(line, square), 0.0), axis=1, keepdims=True)
        weights.append(jnp.concatenate([upright] * PIECES, 0))

    acc[...] = jnp.zeros_like(acc)
    block_rows = 4 * planes * capacity

    def pass_on(k):
        for copy in z_in[k]:
            copy.wait_recv()
        came = rows_in.at[0, 0, rest, lanes(k)]
        y_rest.append(by_chunk(3, k, came, rows_in.at[0, 1, rest, lanes(k)], across))
        b_rest.append(by_chunk(2, k, rows_in.at[0, 0, :, lanes(k)], rows_in.at[1, 0, :, lanes(k)], sibling))

    def take_across(k):
        y_first[k].wait_recv()
        y_rest[k].wait_recv()
        b_across.append(by_chunk(5, k, rows_in.at[0, 1, :, lanes(k)], rows_in.at[1, 1, :, lanes(k)], sibling))

    def multiply(k):
        b_rest[k].wait_recv()
        b_across[k].wait_recv()
        start, size = spans[k]
        for t in range(size // 128):
            tile = rows_in[:, :, :, pl.ds(start + t * 128, 128)]
            loose[t] = tile.reshape(4 * column_rows, 128).astype(f32)
        for p in range(PIECES):
            lhs = jnp.concatenate([
                loose[t, pl.ds(p, block_rows, stride=PIECES), :] for t in range(size // 128)], 1)
            acc[...] += jnp.dot(lhs.astype(bf16), w1[at_piece(p, k), :], preferred_element_type=f32)

    for k in range(chunks):
        pass_on(k)
        if k >= 1:
            take_across(k - 1)
    take_across(chunks - 1)
    for load in loads:
        load.wait()
    for k in range(chunks):
        multiply(k)

    gate_act = acc[:, :hidden_units]
    hidden = (gate_act / (1.0 + jnp.exp(-gate_act)) * acc[:, hidden_units:]).astype(bf16)

    p_out, y_out, z_out = [], [], []

    def stage_a(k):
        start, size = spans[k]
        for p in range(PIECES):
            result = jnp.dot(hidden, wd[:, at_piece(p, k)], preferred_element_type=f32)
            for t in range(size // 128):
                product[start // 128 + t, pl.ds(p, block_rows, stride=PIECES), :] = result[:, t * 128:(t + 1) * 128]
        for t in range(size // 128):
            ps[:, pl.ds(start + t * 128, 128)] = product[
                start // 128 + t, pl.ds(2 * column_rows, 2 * column_rows), :].astype(bf16)
        p_out.append(by_chunk(6, k, ps.at[:, lanes(k)], pr.at[:, lanes(k)], sibling))

    def stage_b(k):
        p_out[k].wait_recv()
        start, size = spans[k]
        for t in range(size // 128):
            here = pl.ds(start + t * 128, 128)
            total = product[start // 128 + t, pl.ds(0, 2 * column_rows), :] + pr[:, here].astype(f32)
            ys[:, here] = total[column_rows:].astype(bf16)
            keep[:, here] = total[:column_rows]
        y_out.append(by_chunk(7, k, ys.at[:, lanes(k)], yr.at[:, lanes(k)], across))

    def stage_c(k):
        y_out[k].wait_recv()
        zs[:, lanes(k)] = (keep[:, lanes(k)] + yr[:, lanes(k)].astype(f32)).astype(bf16)
        z_out.append([
            send(zs.at[pl.ds(j * pair, pair), lanes(k)], zr.at[pl.ds((planes - j) * pair, pair), lanes(k)],
                 zout_send.at[k, planes - j], zout_recv.at[k, planes - j], plane_at(j))
            for j in range(1, planes)])

    def stage_d(k):
        for copy in z_out[k]:
            copy.wait_recv()
        total = None
        for s in range(planes):
            block = zs[first, lanes(k)] if s == 0 else zr[pl.ds(s * pair, pair), lanes(k)]
            picked = lax.dot_general(
                choose[s * pair:(s + 1) * pair], block, (((0,), (0,)), ((), ())), preferred_element_type=f32)
            total = weights[s] * picked if s == 0 else total + weights[s] * picked
        for p in range(PIECES):
            out_ref[:, at_piece(p, k)] = total[p * row_count:(p + 1) * row_count]

    for k in range(chunks):
        stage_a(k)
        if k >= 1:
            stage_b(k - 1)
    stage_b(chunks - 1)
    for k in range(chunks):
        stage_c(k)
    for k in range(chunks):
        stage_d(k)
    for copy in sent:
        copy.wait_send()


def per_device(hidden_rows, expert_ids, gate_values, expert_block, w_gate, w_up, w_down):
    rows, width = hidden_rows.shape
    planes = lax.axis_size("node") // 2
    units = w_gate.shape[1]
    capacity = rows * expert_ids.shape[1] * 3 // (2 * expert_block.shape[0])
    pair = capacity * PIECES
    piece = width // PIECES
    chunks = len(lane_spans(piece))
    largest = max(size for _, size in lane_spans(piece))
    column = planes * pair
    bf16, f32 = jnp.bfloat16, jnp.float32
    vmem = pl.BlockSpec(memory_space=pltpu.VMEM)
    anywhere = pl.BlockSpec(memory_space=pl.ANY)
    dma = pltpu.SemaphoreType.DMA
    combined = pl.pallas_call(
        functools.partial(routed_kernel, planes, capacity),
        out_shape=jax.ShapeDtypeStruct((rows, width), f32),
        in_specs=[vmem, vmem, pl.BlockSpec(memory_space=pltpu.SMEM), vmem, anywhere, anywhere, anywhere],
        out_specs=vmem,
        scratch_shapes=[
            pltpu.VMEM((width, 2 * units), bf16),
            pltpu.VMEM((units, width), bf16),
            pltpu.VMEM((column, piece), bf16),
            pltpu.VMEM((2, 2, column, piece), bf16),
            pltpu.VMEM((largest // 128, 4 * column, 128), f32),
            pltpu.VMEM((4 * planes * capacity, 2 * units), f32),
            pltpu.VMEM((piece // 128, 4 * column, 128), f32),
            pltpu.VMEM((2 * column, piece), bf16),
            pltpu.VMEM((2 * column, piece), bf16),
            pltpu.VMEM((column, piece), bf16),
            pltpu.VMEM((column, piece), bf16),
            pltpu.VMEM((column, piece), f32),
            pltpu.VMEM((column, piece), bf16),
            pltpu.VMEM((column, piece), bf16),
            dma((3,)),
            dma((8, chunks)),
            dma((8, chunks)),
            dma((chunks, planes)),
            dma((chunks, planes)),
            dma((chunks, planes)),
            dma((chunks, planes)),
        ],
        compiler_params=pltpu.CompilerParams(
            collective_id=0, has_side_effects=True, vmem_limit_bytes=56 * 1024 * 1024),
    )(expert_ids.T, gate_values.T, expert_block, hidden_rows, w_gate, w_up, w_down)
    return combined.astype(bf16)


def solution(mesh):
    placed = (
        P(("groups", "node", "local"), None),
        P(("groups", "node", "local"), None),
        P(("groups", "node", "local"), None),
        P(),
        P(None, ("node", "local")),
        P(None, ("node", "local")),
        P(("node", "local"), None),
    )
    return jax.shard_map(
        per_device,
        mesh=mesh,
        in_specs=placed,
        out_specs=P(("groups", "node", "local"), None),
        check_vma=False,
    )
```
